32 devices in a mesh: seq: 16 (over z, y, x), head: 2 (over core).
Axes of the slice: x: 2, y: 2, z: 4, core: 2. Of those that a mesh axis runs over, the one named last changes fastest.
Arguments:
- queries: bfloat16 [4096, 4096], P('seq', 'head'), may hold values from -6 to 6
- key_rows: bfloat16 [4096, 4096], P('seq', 'head'), may hold values from -6 to 6
- value_rows: bfloat16 [4096, 4096], P('seq', 'head'), may hold values from -6 to 6
- doc_block: int32 [32], P('seq'), may hold values from 0 to 4, never falling along the last dimension, each value on 1 to 16 neighbouring positions
- out_weight: bfloat16 [4096, 4096], P('head'), may hold values from -0.09375 to 0.09375
- grad_output: bfloat16 [4096, 4096], P('seq'), may hold values from -8 to 8
Outputs:
- projected: bfloat16 [4096, 4096], P('seq', 'head')
- grad_queries: bfloat16 [4096, 4096], P('seq', 'head')
- grad_keys: bfloat16 [4096, 4096], P('seq', 'head')
- grad_values: bfloat16 [4096, 4096], P('seq', 'head')
- grad_weight: float32 [4096, 4096], P('head', 'seq')
The draws below stay inside these ranges and needn't reach their ends.
Inputs may be any that keep to these rules, and one draw needn't show every extreme that they name: `doc_block`: document numbers never fall along the blocks; each document covers 1 to 16 blocks, one exactly 16.
All inputs are finite; a program needn't handle non-finite values.
Results may differ from the reference program's by a relative error of at most 0.0061.
Values may be sent and summed in bfloat16 or wider, within the bound.
A program may use at most 192 MiB of HBM per device.

```python
import math
import jax
import jax.numpy as jnp
import numpy as np
from jax import lax

D = 4096
HEADS = 32
HD = 128
BLK = 128
TOKENS = 4096
NBLK = 32
DOCS = 5
MOST = 16
N_HEAD = 2


def raised(result, rng, source, target, shards_of, factor):
    owner, partner = [(jnp.arange(result.shape[axis_at]) // (result.shape[axis_at] // shards_of)).reshape([-1 if axis == axis_at else 1 for axis in range(result.ndim)]) for axis_at in (source, target)]
    chosen = jax.random.permutation(rng, shards_of)[partner]
    strong = (owner == chosen) | (owner == (partner + shards_of // 2) % shards_of)
    return jnp.where(strong, factor * result, result)


def level_of(own_key, shape, shards, smallest, top_value):
    level = 1.0
    for dim, parts in shards:
        heights = jax.random.uniform(jax.random.fold_in(jax.random.fold_in(own_key, 6), dim), (parts,), jnp.float32, smallest / len(shards), top_value / len(shards))
        level = level * jnp.repeat(jnp.exp(heights), shape[dim] // parts).reshape((-1,) + (1,) * (len(shape) - 1 - dim))
    return level


def split_up(count, total, limit, lean):
    portions = [(1 << 20) // math.isqrt(rank ** lean) + 1 for rank in range(2, count + 1)]
    rest, counts = total - limit - (count - 1), [1] * (count - 1)
    while rest > 0:
        candidates = [i for i in range(count - 1) if counts[i] < limit]
        pool, left = sum([portions[i] for i in candidates]), rest
        for i in candidates:
            more = min(limit - counts[i], max(1, left * portions[i] // pool), rest)
            counts[i] = counts[i] + more
            rest = rest - more
    return np.array([limit] + counts)


def uneven(key, amount, total, limit, lean):
    if amount == 2:
        one = jax.random.randint(key, (), max(1, total - limit), min(limit, total - 1) + 1)
        return jnp.stack([one, total - one])
    sizes = jnp.asarray(split_up(amount, total, limit, lean), jnp.int32)
    couples = (amount - 1) // 2
    source_of, sink = sizes[1:1 + 2 * couples:2], sizes[2:2 + 2 * couples:2]
    slack = jnp.minimum(source_of - 1, limit - sink)
    shifted = jax.random.randint(jax.random.fold_in(key, 1), (couples,), 0, 1 << 20) % (slack + 1)
    sizes = sizes.at[1:1 + 2 * couples:2].set(source_of - shifted).at[2:2 + 2 * couples:2].set(sink + shifted)
    return sizes[jax.random.permutation(jax.random.fold_in(key, 2), amount)]


def bell_draw(stream_key, shape, width, bound, pieces=(), held_as=jnp.bfloat16):
    gain = level_of(stream_key, shape, pieces, -0.22, 0.18) if pieces else 1.0
    drawn = jax.random.normal(stream_key, shape, jnp.float32) * width * gain
    return jnp.minimum(jnp.maximum(drawn, -bound), bound).astype(held_as)


def noise_with(rng, extent, width, limit, split, heavy, kind=jnp.bfloat16):
    entries = width * jax.random.normal(rng, extent, jnp.float32)
    if split:
        entries = entries * level_of(rng, extent, split, -0.22, 0.18)
    return jnp.clip(raised(entries, jax.random.fold_in(rng, 3), *heavy), -limit, limit).astype(kind)


def setup_inputs(seed: int = 0) -> dict:
    keys = jax.random.split(jax.random.key(seed), 7)
    return {
        "queries": bell_draw(keys[0], (TOKENS, HEADS * HD), 1.0, 6.0, ((0, 16), (1, 2))),
        "key_rows": bell_draw(keys[1], (TOKENS, HEADS * HD), 1.0, 6.0, ((0, 16), (1, 2))),
        "value_rows": bell_draw(keys[2], (TOKENS, HEADS * HD), 1.0, 6.0, ((0, 16), (1, 2))),
        "doc_block": jnp.searchsorted(jnp.cumsum(uneven(keys[3], DOCS, NBLK, MOST, 2)), jnp.arange(NBLK), side="right").astype(jnp.int32),
        "out_weight": bell_draw(keys[4], (HEADS * HD, D), (HEADS * HD) ** -0.5, 0.09375, ((0, 2),)),
        "grad_output": noise_with(keys[5], (TOKENS, D), 1.0, 8.0, ((0, 16),), (0, 1, 16, 2.0)),
    }


def reference(queries, key_rows, value_rows, doc_block, out_weight, grad_output):
    hi = lax.Precision.HIGHEST
    factor = 1.0 / HD
    def blocks(array):
        return array.astype(jnp.float32).reshape(NBLK, BLK, HEADS, HD)
    query_blocks = blocks(queries)
    key_blocks = blocks(key_rows)
    value_blocks = blocks(value_rows)
    causal = jnp.tril(jnp.ones((BLK, BLK), dtype=bool))
    scores = jnp.einsum('nthd,nshd->nhts', query_blocks, key_blocks, precision=hi) * factor
    probs = jnp.where(causal, scores, 0.0).astype(jnp.bfloat16)
    probs_wide = probs.astype(jnp.float32)
    block_states = jnp.einsum('nshd,nshe->nhde', key_blocks, value_blocks, precision=hi)
    positions = jnp.arange(NBLK, dtype=jnp.int32)
    same_doc = doc_block[:, None] == doc_block[None, :]
    earlier = (same_doc & (positions[None, :] < positions[:, None])).astype(jnp.float32)
    later = (same_doc & (positions[None, :] > positions[:, None])).astype(jnp.float32)
    before = jnp.einsum('bc,chde->bhde', earlier, block_states, precision=hi)
    attended = jnp.einsum('nhts,nshe->nthe', probs_wide, value_blocks, precision=hi)
    attended = attended + factor * jnp.einsum('nthd,nhde->nthe', query_blocks, before, precision=hi)
    attended = attended.astype(jnp.bfloat16).reshape(TOKENS, HEADS * HD)
    group = HEADS * HD // N_HEAD
    total = jnp.zeros((TOKENS, D), jnp.float32)
    for index_g in range(N_HEAD):
        part = jnp.dot(attended[:, index_g * group:(index_g + 1) * group], out_weight[index_g * group:(index_g + 1) * group], preferred_element_type=jnp.float32)
        part = lax.optimization_barrier(part.astype(jnp.bfloat16))
        total = total + part.astype(jnp.float32)
    projected = total.astype(jnp.bfloat16)
    grad_att = lax.dot_general(grad_output, out_weight, (((1,), (1,)), ((), ())), preferred_element_type=jnp.float32).astype(jnp.bfloat16)
    grad_blocks = grad_att.astype(jnp.float32).reshape(NBLK, BLK, HEADS, HD)
    grad_scores = jnp.einsum('nthe,nshe->nhts', grad_blocks, value_blocks, precision=hi) * factor
    grad_probs = jnp.where(causal, grad_scores, 0.0).astype(jnp.bfloat16).astype(jnp.float32)
    grad_states = jnp.einsum('nthd,nthe->nhde', query_blocks, grad_blocks, precision=hi)
    after = jnp.einsum('bc,chde->bhde', later, grad_states, precision=hi)
    grad_queries = jnp.einsum('nhts,nshd->nthd', grad_probs, key_blocks, precision=hi) + factor * jnp.einsum('nthe,nhde->nthd', grad_blocks, before, precision=hi)
    grad_keys = jnp.einsum('nhts,nthd->nshd', grad_probs, query_blocks, precision=hi) + factor * jnp.einsum('nshe,nhde->nshd', value_blocks, after, precision=hi)
    grad_values = jnp.einsum('nhts,nthe->nshe', probs_wide, grad_blocks, precision=hi) + factor * jnp.einsum('nshd,nhde->nshe', key_blocks, after, precision=hi)
    grad_weight = lax.dot_general(attended, grad_output, (((0,), (0,)), ((), ())), preferred_element_type=jnp.float32)
    shape_out = (TOKENS, HEADS * HD)
    return (projected, grad_queries.astype(jnp.bfloat16).reshape(shape_out), grad_keys.astype(jnp.bfloat16).reshape(shape_out), grad_values.astype(jnp.bfloat16).reshape(shape_out), grad_weight)
```

```python
import jax
import jax.numpy as jnp
from jax import lax
from jax.sharding import PartitionSpec as P

HD = 128
BLK = 128


def row_groups(count):
    near = 1
    while near * near < count:
        near += 1
    while count % near:
        near += 1
    far = count // near
    rows = [[r * near + c for c in range(near)] for r in range(far)]
    columns = [[r * near + c for r in range(far)] for c in range(near)]
    return near, far, rows, columns


def over_blocks(mask, states):
    count = states.shape[0]
    picked = [
        sum(mask[b, c] * states[c] for c in range(count) if c != b) + jnp.zeros_like(states[0])
        for b in range(count)
    ]
    return jnp.stack(picked)


def carried(states, grads, first_doc, last_doc):
    count, mine = (lax.axis_size("seq"), lax.axis_index("seq"))
    ends = lax.all_gather(jnp.stack([first_doc, last_doc]), "seq")
    firsts, lasts = (ends[:, 0], ends[:, 1])
    heads = states.shape[0]
    rows = heads * HD // count
    both = jnp.stack([states, grads]).astype(jnp.bfloat16).reshape(2, count, rows, HD)
    both = jnp.moveaxis(both, 1, 0)
    got = lax.all_to_all(both, "seq", 0, 0).astype(jnp.float32)
    place = jnp.arange(count)
    ahead = ((lasts[None, :] == firsts[:, None]) & (place[None, :] < place[:, None])).astype(jnp.float32)
    behind = ((firsts[None, :] == lasts[:, None]) & (place[None, :] > place[:, None])).astype(jnp.float32)
    masks = jnp.stack([ahead, behind])
    summed = [jnp.sum(masks[:, j, :].T[:, :, None, None] * got, axis=0) for j in range(count)]
    summed = jnp.stack(summed).astype(jnp.bfloat16)
    back = lax.all_to_all(summed, "seq", 0, 0)
    back = jnp.moveaxis(back, 0, 1).reshape(2, heads, HD, HD).astype(jnp.float32)
    return back[0], back[1]


def body(queries, key_rows, value_rows, doc_block, out_weight, grad_output):
    factor = 1.0 / HD
    tokens_here = queries.shape[0]
    width_here = queries.shape[1]
    heads_here = width_here // HD
    block_count = tokens_here // BLK
    query_blocks = queries.reshape(block_count, BLK, heads_here, HD)
    key_blocks = key_rows.reshape(block_count, BLK, heads_here, HD)
    value_blocks = value_rows.reshape(block_count, BLK, heads_here, HD)
    near, far, rows, columns = row_groups(lax.axis_size("seq"))
    near_out = lax.all_to_all(
        grad_output.reshape(tokens_here, far, near, -1), "seq", 2, 0, axis_index_groups=rows
    ).reshape(near * tokens_here, -1)
    causal = jnp.tril(jnp.ones((BLK, BLK), dtype=bool))
    scores = (
        jnp.einsum("nthd,nshd->nhts", query_blocks, key_blocks, preferred_element_type=jnp.float32)
        * factor
    )
    probs = jnp.where(causal, scores, 0.0).astype(jnp.bfloat16)
    block_states = jnp.einsum(
        "nshd,nshe->nhde", key_blocks, value_blocks, preferred_element_type=jnp.float32
    )
    grad_att = lax.dot_general(
        grad_output, out_weight, (((1,), (1,)), ((), ())), preferred_element_type=jnp.float32
    ).astype(jnp.bfloat16)
    grad_blocks = grad_att.reshape(block_count, BLK, heads_here, HD)
    grad_states = jnp.einsum(
        "nthd,nthe->nhde", query_blocks, grad_blocks, preferred_element_type=jnp.float32
    )
    positions = jnp.arange(block_count, dtype=jnp.int32)
    same_doc = doc_block[:, None] == doc_block[None, :]
    earlier = (same_doc & (positions[None, :] < positions[:, None])).astype(jnp.float32)
    later = (same_doc & (positions[None, :] > positions[:, None])).astype(jnp.float32)
    last_doc = doc_block[block_count - 1]
    first_doc = doc_block[0]
    own_state = jnp.sum(
        jnp.where((doc_block == last_doc)[:, None, None, None], block_states, 0.0), axis=0
    )
    own_grad = jnp.sum(
        jnp.where((doc_block == first_doc)[:, None, None, None], grad_states, 0.0), axis=0
    )
    carry_state, carry_grad = carried(own_state, own_grad, first_doc, last_doc)
    before = over_blocks(earlier, block_states)
    before = before + jnp.where(
        (doc_block == first_doc)[:, None, None, None], carry_state[None], 0.0
    )
    after = over_blocks(later, grad_states)
    after = after + jnp.where((doc_block == last_doc)[:, None, None, None], carry_grad[None], 0.0)
    before = before.astype(jnp.bfloat16)
    after = after.astype(jnp.bfloat16)
    attended = jnp.einsum(
        "nhts,nshe->nthe", probs, value_blocks, preferred_element_type=jnp.float32
    )
    attended = attended + factor * jnp.einsum("nthd,nhde->nthe", query_blocks, before, preferred_element_type=jnp.float32)
    attended = attended.astype(jnp.bfloat16).reshape(tokens_here, width_here)
    partial_value = jnp.dot(attended, out_weight, preferred_element_type=jnp.float32)
    partial_value = lax.optimization_barrier(partial_value.astype(jnp.bfloat16))
    projected = lax.psum_scatter(
        partial_value.astype(jnp.float32).astype(jnp.bfloat16),
        "head",
        scatter_dimension=1,
        tiled=True,
    )
    near_att = lax.all_gather(attended, "seq", axis_index_groups=rows, tiled=True)
    weight_term = lax.dot_general(
        near_att, near_out, (((0,), (0,)), ((), ())), preferred_element_type=jnp.float32
    ).astype(jnp.bfloat16)
    weight_parts = lax.all_to_all(
        weight_term.reshape(width_here, far, -1),
        "seq",
        1,
        0,
        axis_index_groups=columns,
    )
    grad_weight = jnp.sum(weight_parts.astype(jnp.float32), axis=0)
    grad_scores = (
        jnp.einsum("nthe,nshe->nhts", grad_blocks, value_blocks, preferred_element_type=jnp.float32)
        * factor
    )
    grad_probs = jnp.where(causal, grad_scores, 0.0).astype(jnp.bfloat16)
    grad_queries = jnp.einsum(
        "nhts,nshd->nthd", grad_probs, key_blocks, preferred_element_type=jnp.float32
    )
    grad_queries = grad_queries + factor * jnp.einsum(
        "nthe,nhde->nthd", grad_blocks, before, preferred_element_type=jnp.float32
    )
    grad_keys = jnp.einsum(
        "nhts,nthd->nshd", grad_probs, query_blocks, preferred_element_type=jnp.float32
    )
    grad_keys = grad_keys + factor * jnp.einsum(
        "nshe,nhde->nshd", value_blocks, after, preferred_element_type=jnp.float32
    )
    grad_values = jnp.einsum(
        "nhts,nthe->nshe", probs, grad_blocks, preferred_element_type=jnp.float32
    )
    grad_values = grad_values + factor * jnp.einsum(
        "nshd,nhde->nshe", key_blocks, after, preferred_element_type=jnp.float32
    )
    shape_out = (tokens_here, width_here)
    return (
        projected,
        grad_queries.astype(jnp.bfloat16).reshape(shape_out),
        grad_keys.astype(jnp.bfloat16).reshape(shape_out),
        grad_values.astype(jnp.bfloat16).reshape(shape_out),
        grad_weight,
    )


def solution(mesh):
    placed = (
        P("seq", "head"),
        P("seq", "head"),
        P("seq", "head"),
        P("seq"),
        P("head", None),
        P("seq", None),
    )
    return jax.shard_map(
        body,
        mesh=mesh,
        in_specs=placed,
        out_specs=(
            P("seq", "head"),
            P("seq", "head"),
            P("seq", "head"),
            P("seq", "head"),
            P("head", "seq"),
        ),
        check_vma=False,
    )
```

```python
import jax
import jax.numpy as jnp
from jax import lax
from jax.sharding import PartitionSpec as P

HD = 128
BLK = 128


def row_groups(count):
    near = 1
    while near * near < count:
        near += 1
    while count % near:
        near += 1
    far = count // near
    return near, far


def swapped(near, far, step):
    return [(r * near + c, r * near + (c ^ step)) for r in range(far) for c in range(near)]


def column_sum(term, near, far):
    row = lax.axis_index("seq") // near
    wide = term.shape[1] // far

    def block(place):
        start = jnp.clip(place, 0, far - 1) * wide
        return lax.dynamic_slice_in_dim(term, start, wide, 1)

    up, down = (None, None)
    for step in range(1, far):
        climb = block(row + far - step)
        sink = block(row - far + step)
        if step > 1:
            climb = climb + up.astype(jnp.float32)
            sink = sink + down.astype(jnp.float32)
        rising = [(r * near + c, (r + 1) * near + c) for r in range(step) for c in range(near)]
        falling = [
            ((far - 1 - r) * near + c, (far - 2 - r) * near + c)
            for r in range(step)
            for c in range(near)
        ]
        up = lax.ppermute(climb.astype(jnp.bfloat16), "seq", rising)
        down = lax.ppermute(sink.astype(jnp.bfloat16), "seq", falling)
    return block(row) + up.astype(jnp.float32) + down.astype(jnp.float32)


def over_blocks(mask, states):
    count = states.shape[0]
    picked = [
        sum(mask[b, c] * states[c] for c in range(count) if c != b) + jnp.zeros_like(states[0])
        for b in range(count)
    ]
    return jnp.stack(picked)


def carried(states, grads, first_doc, last_doc):
    count, mine = (lax.axis_size("seq"), lax.axis_index("seq"))
    ends = lax.all_to_all(
        jnp.broadcast_to(jnp.stack([first_doc, last_doc]), (count, 2)), "seq", 0, 0
    )
    firsts, lasts = (ends[:, 0], ends[:, 1])
    heads = states.shape[0]
    rows = heads * HD // count
    both = jnp.stack([states, grads]).astype(jnp.bfloat16).reshape(2, count, rows, HD)
    both = jnp.moveaxis(both, 1, 0)
    got = lax.all_to_all(both, "seq", 0, 0).astype(jnp.float32)
    place = jnp.arange(count)
    ahead = ((lasts[None, :] == firsts[:, None]) & (place[None, :] < place[:, None])).astype(jnp.float32)
    behind = ((firsts[None, :] == lasts[:, None]) & (place[None, :] > place[:, None])).astype(jnp.float32)
    masks = jnp.stack([ahead, behind])
    summed = [jnp.sum(masks[:, j, :].T[:, :, None, None] * got, axis=0) for j in range(count)]
    summed = jnp.stack(summed).astype(jnp.bfloat16)
    back = lax.all_to_all(summed, "seq", 0, 0)
    back = jnp.moveaxis(back, 0, 1).reshape(2, heads, HD, HD).astype(jnp.float32)
    return back[0], back[1]


def body(queries, key_rows, value_rows, doc_block, out_weight, grad_output):
    factor = 1.0 / HD
    tokens_here = queries.shape[0]
    width_here = queries.shape[1]
    heads_here = width_here // HD
    block_count = tokens_here // BLK
    query_blocks = queries.reshape(block_count, BLK, heads_here, HD)
    key_blocks = key_rows.reshape(block_count, BLK, heads_here, HD)
    value_blocks = value_rows.reshape(block_count, BLK, heads_here, HD)
    near, far = row_groups(lax.axis_size("seq"))
    seat = lax.axis_index("seq") % near
    out_parts = grad_output.reshape(tokens_here, far, near, -1)

    def out_part(place):
        part = lax.dynamic_index_in_dim(out_parts, place, 2, keepdims=False)
        return part.reshape(tokens_here, -1)

    near_out = [out_part(seat)]
    for step in range(1, near):
        near_out.append(lax.ppermute(out_part(seat ^ step), "seq", swapped(near, far, step)))
    causal = jnp.tril(jnp.ones((BLK, BLK), dtype=bool))
    scores = (
        jnp.einsum("nthd,nshd->nhts", query_blocks, key_blocks, preferred_element_type=jnp.float32)
        * factor
    )
    probs = jnp.where(causal, scores, 0.0).astype(jnp.bfloat16)
    block_states = jnp.einsum(
        "nshd,nshe->nhde", key_blocks, value_blocks, preferred_element_type=jnp.float32
    )
    grad_att = lax.dot_general(
        grad_output, out_weight, (((1,), (1,)), ((), ())), preferred_element_type=jnp.float32
    ).astype(jnp.bfloat16)
    grad_blocks = grad_att.reshape(block_count, BLK, heads_here, HD)
    grad_states = jnp.einsum(
        "nthd,nthe->nhde", query_blocks, grad_blocks, preferred_element_type=jnp.float32
    )
    positions = jnp.arange(block_count, dtype=jnp.int32)
    same_doc = doc_block[:, None] == doc_block[None, :]
    earlier = (same_doc & (positions[None, :] < positions[:, None])).astype(jnp.float32)
    later = (same_doc & (positions[None, :] > positions[:, None])).astype(jnp.float32)
    last_doc = doc_block[block_count - 1]
    first_doc = doc_block[0]
    own_state = jnp.sum(
        jnp.where((doc_block == last_doc)[:, None, None, None], block_states, 0.0), axis=0
    )
    own_grad = jnp.sum(
        jnp.where((doc_block == first_doc)[:, None, None, None], grad_states, 0.0), axis=0
    )
    carry_state, carry_grad = carried(own_state, own_grad, first_doc, last_doc)
    before = over_blocks(earlier, block_states)
    before = before + jnp.where(
        (doc_block == first_doc)[:, None, None, None], carry_state[None], 0.0
    )
    after = over_blocks(later, grad_states)
    after = after + jnp.where((doc_block == last_doc)[:, None, None, None], carry_grad[None], 0.0)
    before = before.astype(jnp.bfloat16)
    after = after.astype(jnp.bfloat16)
    attended = jnp.einsum(
        "nhts,nshe->nthe", probs, value_blocks, preferred_element_type=jnp.float32
    )
    attended = attended + factor * jnp.einsum("nthd,nhde->nthe", query_blocks, before, preferred_element_type=jnp.float32)
    attended = attended.astype(jnp.bfloat16).reshape(tokens_here, width_here)
    partial_value = jnp.dot(attended, out_weight, preferred_element_type=jnp.float32)
    partial_value = lax.optimization_barrier(partial_value.astype(jnp.bfloat16))
    projected = lax.psum_scatter(
        partial_value.astype(jnp.float32).astype(jnp.bfloat16),
        "head",
        scatter_dimension=1,
        tiled=True,
    )
    near_att = [attended]
    for step in range(1, near):
        near_att.append(lax.ppermute(attended, "seq", swapped(near, far, step)))
    half = near // 2
    weight_term = sum(
        lax.dot_general(
            jnp.concatenate(near_att[at : at + half]),
            jnp.concatenate(near_out[at : at + half]),
            (((0,), (0,)), ((), ())),
            preferred_element_type=jnp.float32,
        )
        for at in range(0, near, half)
    )
    grad_weight = column_sum(weight_term, near, far)
    grad_scores = (
        jnp.einsum("nthe,nshe->nhts", grad_blocks, value_blocks, preferred_element_type=jnp.float32)
        * factor
    )
    grad_probs = jnp.where(causal, grad_scores, 0.0).astype(jnp.bfloat16)
    grad_queries = jnp.einsum(
        "nhts,nshd->nthd", grad_probs, key_blocks, preferred_element_type=jnp.float32
    )
    grad_queries = grad_queries + factor * jnp.einsum(
        "nthe,nhde->nthd", grad_blocks, before, preferred_element_type=jnp.float32
    )
    grad_keys = jnp.einsum(
        "nhts,nthd->nshd", grad_probs, query_blocks, preferred_element_type=jnp.float32
    )
    grad_keys = grad_keys + factor * jnp.einsum(
        "nshe,nhde->nshd", value_blocks, after, preferred_element_type=jnp.float32
    )
    grad_values = jnp.einsum(
        "nhts,nthe->nshe", probs, grad_blocks, preferred_element_type=jnp.float32
    )
    grad_values = grad_values + factor * jnp.einsum(
        "nshd,nhde->nshe", key_blocks, after, preferred_element_type=jnp.float32
    )
    shape_out = (tokens_here, width_here)
    return (
        projected,
        grad_queries.astype(jnp.bfloat16).reshape(shape_out),
        grad_keys.astype(jnp.bfloat16).reshape(shape_out),
        grad_values.astype(jnp.bfloat16).reshape(shape_out),
        grad_weight,
    )


def solution(mesh):
    placed = (
        P("seq", "head"),
        P("seq", "head"),
        P("seq", "head"),
        P("seq"),
        P("head", None),
        P("seq", None),
    )
    return jax.shard_map(
        body,
        mesh=mesh,
        in_specs=placed,
        out_specs=(
            P("seq", "head"),
            P("seq", "head"),
            P("seq", "head"),
            P("seq", "head"),
            P("head", "seq"),
        ),
        check_vma=False,
    )
```

```python
import jax
import jax.numpy as jnp
from jax import lax
from jax.sharding import PartitionSpec as P

HD = 128
BLK = 128


def row_groups(count):
    near = 1
    while near * near < count:
        near += 1
    while count % near:
        near += 1
    far = count // near
    return near, far


def swapped(near, far, step):
    return [(r * near + c, r * near + (c ^ step)) for r in range(far) for c in range(near)]


def over_blocks(mask, states):
    count = states.shape[0]
    picked = [
        sum(mask[b, c] * states[c] for c in range(count) if c != b) + jnp.zeros_like(states[0])
        for b in range(count)
    ]
    return jnp.stack(picked)


def carried(states, grads, first_doc, last_doc):
    count, mine = (lax.axis_size("seq"), lax.axis_index("seq"))
    ends = lax.all_to_all(
        jnp.broadcast_to(jnp.stack([first_doc, last_doc]), (count, 2)), "seq", 0, 0
    )
    firsts, lasts = (ends[:, 0], ends[:, 1])
    heads = states.shape[0]
    rows = heads * HD // count
    both = jnp.stack([states, grads]).astype(jnp.bfloat16).reshape(2, count, rows, HD)
    both = jnp.moveaxis(both, 1, 0)
    got = lax.all_to_all(both, "seq", 0, 0).astype(jnp.float32)
    place = jnp.arange(count)
    ahead = ((lasts[None, :] == firsts[:, None]) & (place[None, :] < place[:, None])).astype(jnp.float32)
    behind = ((firsts[None, :] == lasts[:, None]) & (place[None, :] > place[:, None])).astype(jnp.float32)
    masks = jnp.stack([ahead, behind])
    summed = [jnp.sum(masks[:, j, :].T[:, :, None, None] * got, axis=0) for j in range(count)]
    summed = jnp.stack(summed).astype(jnp.bfloat16)
    back = lax.all_to_all(summed, "seq", 0, 0)
    back = jnp.moveaxis(back, 0, 1).reshape(2, heads, HD, HD).astype(jnp.float32)
    return back[0], back[1]


def body(queries, key_rows, value_rows, doc_block, out_weight, grad_output):
    factor = 1.0 / HD
    tokens_here = queries.shape[0]
    width_here = queries.shape[1]
    heads_here = width_here // HD
    block_count = tokens_here // BLK
    query_blocks = queries.reshape(block_count, BLK, heads_here, HD)
    key_blocks = key_rows.reshape(block_count, BLK, heads_here, HD)
    value_blocks = value_rows.reshape(block_count, BLK, heads_here, HD)
    near, far = row_groups(lax.axis_size("seq"))
    seat = lax.axis_index("seq") % near
    out_parts = grad_output.reshape(tokens_here, far, near, -1)

    def out_part(place):
        part = lax.dynamic_index_in_dim(out_parts, place, 2, keepdims=False)
        return part.reshape(tokens_here, -1)

    near_out = [out_part(seat)]
    for step in range(1, near):
        near_out.append(lax.ppermute(out_part(seat ^ step), "seq", swapped(near, far, step)))
    causal = jnp.tril(jnp.ones((BLK, BLK), dtype=bool))
    scores = (
        jnp.einsum("nthd,nshd->nhts", query_blocks, key_blocks, preferred_element_type=jnp.float32)
        * factor
    )
    probs = jnp.where(causal, scores, 0.0).astype(jnp.bfloat16)
    block_states = jnp.einsum(
        "nshd,nshe->nhde", key_blocks, value_blocks, preferred_element_type=jnp.float32
    )
    grad_att = lax.dot_general(
        grad_output, out_weight, (((1,), (1,)), ((), ())), preferred_element_type=jnp.float32
    ).astype(jnp.bfloat16)
    grad_blocks = grad_att.reshape(block_count, BLK, heads_here, HD)
    grad_states = jnp.einsum(
        "nthd,nthe->nhde", query_blocks, grad_blocks, preferred_element_type=jnp.float32
    )
    positions = jnp.arange(block_count, dtype=jnp.int32)
    same_doc = doc_block[:, None] == doc_block[None, :]
    earlier = (same_doc & (positions[None, :] < positions[:, None])).astype(jnp.float32)
    later = (same_doc & (positions[None, :] > positions[:, None])).astype(jnp.float32)
    last_doc = doc_block[block_count - 1]
    first_doc = doc_block[0]
    own_state = jnp.sum(
        jnp.where((doc_block == last_doc)[:, None, None, None], block_states, 0.0), axis=0
    )
    own_grad = jnp.sum(
        jnp.where((doc_block == first_doc)[:, None, None, None], grad_states, 0.0), axis=0
    )
    own_state, own_grad, near_out = lax.optimization_barrier((own_state, own_grad, near_out))
    carry_state, carry_grad = carried(own_state, own_grad, first_doc, last_doc)
    before = over_blocks(earlier, block_states)
    before = before + jnp.where(
        (doc_block == first_doc)[:, None, None, None], carry_state[None], 0.0
    )
    after = over_blocks(later, grad_states)
    after = after + jnp.where((doc_block == last_doc)[:, None, None, None], carry_grad[None], 0.0)
    before = before.astype(jnp.bfloat16)
    after = after.astype(jnp.bfloat16)
    attended = jnp.einsum(
        "nhts,nshe->nthe", probs, value_blocks, preferred_element_type=jnp.float32
    )
    attended = attended + factor * jnp.einsum("nthd,nhde->nthe", query_blocks, before, preferred_element_type=jnp.float32)
    attended = attended.astype(jnp.bfloat16).reshape(tokens_here, width_here)
    partial_value = jnp.dot(attended, out_weight, preferred_element_type=jnp.float32)
    partial_value = lax.optimization_barrier(partial_value.astype(jnp.bfloat16))
    projected = lax.psum_scatter(
        partial_value.astype(jnp.float32).astype(jnp.bfloat16),
        "head",
        scatter_dimension=1,
        tiled=True,
    )
    columns = [[r * near + c for r in range(far)] for c in range(near)]
    rows = [[r * near + c for c in range(near)] for r in range(far)]
    near_out = jnp.stack(near_out)
    near_out = jnp.concatenate(
        [lax.dynamic_index_in_dim(near_out, seat ^ c, 0, keepdims=False) for c in range(near)]
    )
    half = width_here // 2
    halves = []
    for at in (0, half):
        near_att = lax.all_gather(
            attended[:, at : at + half], "seq", axis_index_groups=rows, tiled=True
        )
        weight_term = lax.dot_general(
            near_att, near_out, (((0,), (0,)), ((), ())), preferred_element_type=jnp.float32
        ).astype(jnp.bfloat16)
        weight_parts = lax.all_to_all(
            weight_term.reshape(half, far, -1), "seq", 1, 0, axis_index_groups=columns
        )
        halves.append(jnp.sum(weight_parts.astype(jnp.float32), axis=0))
    grad_weight = jnp.concatenate(halves)
    grad_scores = (
        jnp.einsum("nthe,nshe->nhts", grad_blocks, value_blocks, preferred_element_type=jnp.float32)
        * factor
    )
    grad_probs = jnp.where(causal, grad_scores, 0.0).astype(jnp.bfloat16)
    grad_queries = jnp.einsum(
        "nhts,nshd->nthd", grad_probs, key_blocks, preferred_element_type=jnp.float32
    )
    grad_queries = grad_queries + factor * jnp.einsum(
        "nthe,nhde->nthd", grad_blocks, before, preferred_element_type=jnp.float32
    )
    grad_keys = jnp.einsum(
        "nhts,nthd->nshd", grad_probs, query_blocks, preferred_element_type=jnp.float32
    )
    grad_keys = grad_keys + factor * jnp.einsum(
        "nshe,nhde->nshd", value_blocks, after, preferred_element_type=jnp.float32
    )
    grad_values = jnp.einsum(
        "nhts,nthe->nshe", probs, grad_blocks, preferred_element_type=jnp.float32
    )
    grad_values = grad_values + factor * jnp.einsum(
        "nshd,nhde->nshe", key_blocks, after, preferred_element_type=jnp.float32
    )
    shape_out = (tokens_here, width_here)
    return (
        projected,
        grad_queries.astype(jnp.bfloat16).reshape(shape_out),
        grad_keys.astype(jnp.bfloat16).reshape(shape_out),
        grad_values.astype(jnp.bfloat16).reshape(shape_out),
        grad_weight,
    )


def solution(mesh):
    placed = (
        P("seq", "head"),
        P("seq", "head"),
        P("seq", "head"),
        P("seq"),
        P("head", None),
        P("seq", None),
    )
    return jax.shard_map(
        body,
        mesh=mesh,
        in_specs=placed,
        out_specs=(
            P("seq", "head"),
            P("seq", "head"),
            P("seq", "head"),
            P("seq", "head"),
            P("head", "seq"),
        ),
        check_vma=False,
    )
```

```python
import jax
import jax.numpy as jnp
from jax import lax
from jax.sharding import PartitionSpec as P

HD = 128
BLK = 128


def row_groups(count):
    near = 1
    while near * near < count:
        near += 1
    while count % near:
        near += 1
    far = count // near
    return near, far


def swapped(near, far, step):
    return [(r * near + c, r * near + (c ^ step)) for r in range(far) for c in range(near)]


def over_blocks(mask, states):
    count = states.shape[0]
    picked = [
        sum(mask[b, c] * states[c] for c in range(count) if c != b) + jnp.zeros_like(states[0])
        for b in range(count)
    ]
    return jnp.stack(picked)


def carried(states, grads, first_doc, last_doc):
    count, mine = (lax.axis_size("seq"), lax.axis_index("seq"))
    ends = lax.all_to_all(
        jnp.broadcast_to(jnp.stack([first_doc, last_doc]), (count, 2)), "seq", 0, 0
    )
    firsts, lasts = (ends[:, 0], ends[:, 1])
    heads = states.shape[0]
    rows = heads * HD // count
    both = jnp.stack([states, grads]).astype(jnp.bfloat16).reshape(2, count, rows, HD)
    both = jnp.moveaxis(both, 1, 0)
    got = lax.all_to_all(both, "seq", 0, 0)
    place = jnp.arange(count)
    ahead = ((lasts[None, :] == firsts[:, None]) & (place[None, :] < place[:, None])).astype(jnp.float32)
    behind = ((firsts[None, :] == lasts[:, None]) & (place[None, :] > place[:, None])).astype(jnp.float32)
    masks = jnp.stack([ahead, behind])
    summed = jnp.einsum(
        "kji,ikrd->jkrd", masks.astype(jnp.bfloat16), got, preferred_element_type=jnp.float32
    ).astype(jnp.bfloat16)
    back = lax.all_to_all(summed, "seq", 0, 0)
    back = jnp.moveaxis(back, 0, 1).reshape(2, heads, HD, HD).astype(jnp.float32)
    return back[0], back[1]


def body(queries, key_rows, value_rows, doc_block, out_weight, grad_output):
    factor = 1.0 / HD
    tokens_here = queries.shape[0]
    width_here = queries.shape[1]
    heads_here = width_here // HD
    block_count = tokens_here // BLK
    query_blocks = queries.reshape(block_count, BLK, heads_here, HD)
    key_blocks = key_rows.reshape(block_count, BLK, heads_here, HD)
    value_blocks = value_rows.reshape(block_count, BLK, heads_here, HD)
    near, far = row_groups(lax.axis_size("seq"))
    seat = lax.axis_index("seq") % near
    out_parts = grad_output.reshape(tokens_here, far, near, -1)

    def out_part(place):
        part = lax.dynamic_index_in_dim(out_parts, place, 2, keepdims=False)
        return part.reshape(tokens_here, -1)

    near_out = [out_part(seat)]
    for step in range(1, near):
        near_out.append(lax.ppermute(out_part(seat ^ step), "seq", swapped(near, far, step)))
    causal = jnp.tril(jnp.ones((BLK, BLK), dtype=bool))
    scores = (
        jnp.einsum("nthd,nshd->nhts", query_blocks, key_blocks, preferred_element_type=jnp.float32)
        * factor
    )
    probs = jnp.where(causal, scores, 0.0).astype(jnp.bfloat16)
    block_states = jnp.einsum(
        "nshd,nshe->nhde", key_blocks, value_blocks, preferred_element_type=jnp.float32
    )
    grad_att = lax.dot_general(
        grad_output, out_weight, (((1,), (1,)), ((), ())), preferred_element_type=jnp.float32
    ).astype(jnp.bfloat16)
    grad_blocks = grad_att.reshape(block_count, BLK, heads_here, HD)
    grad_states = jnp.einsum(
        "nthd,nthe->nhde", query_blocks, grad_blocks, preferred_element_type=jnp.float32
    )
    positions = jnp.arange(block_count, dtype=jnp.int32)
    same_doc = doc_block[:, None] == doc_block[None, :]
    earlier = (same_doc & (positions[None, :] < positions[:, None])).astype(jnp.float32)
    later = (same_doc & (positions[None, :] > positions[:, None])).astype(jnp.float32)
    last_doc = doc_block[block_count - 1]
    first_doc = doc_block[0]
    own_state = jnp.sum(
        jnp.where((doc_block == last_doc)[:, None, None, None], block_states, 0.0), axis=0
    )
    own_grad = jnp.sum(
        jnp.where((doc_block == first_doc)[:, None, None, None], grad_states, 0.0), axis=0
    )
    own_state, own_grad, near_out = lax.optimization_barrier((own_state, own_grad, near_out))
    carry_state, carry_grad = carried(own_state, own_grad, first_doc, last_doc)
    before = over_blocks(earlier, block_states)
    before = before + jnp.where(
        (doc_block == first_doc)[:, None, None, None], carry_state[None], 0.0
    )
    after = over_blocks(later, grad_states)
    after = after + jnp.where((doc_block == last_doc)[:, None, None, None], carry_grad[None], 0.0)
    before = before.astype(jnp.bfloat16)
    after = after.astype(jnp.bfloat16)
    attended = jnp.einsum(
        "nhts,nshe->nthe", probs, value_blocks, preferred_element_type=jnp.float32
    )
    attended = attended + factor * jnp.einsum("nthd,nhde->nthe", query_blocks, before, preferred_element_type=jnp.float32)
    attended = attended.astype(jnp.bfloat16).reshape(tokens_here, width_here)
    partial_value = jnp.dot(attended, out_weight, preferred_element_type=jnp.float32)
    partial_value = lax.optimization_barrier(partial_value.astype(jnp.bfloat16))
    projected = lax.psum_scatter(
        partial_value.astype(jnp.float32).astype(jnp.bfloat16),
        "head",
        scatter_dimension=1,
        tiled=True,
    )
    columns = [[r * near + c for r in range(far)] for c in range(near)]
    rows = [[r * near + c for c in range(near)] for r in range(far)]
    near_out = jnp.stack(near_out)
    near_out = jnp.concatenate(
        [lax.dynamic_index_in_dim(near_out, seat ^ c, 0, keepdims=False) for c in range(near)]
    )
    quarter = width_here // 4
    halves = []
    for at, wide in ((0, quarter), (quarter, quarter), (2 * quarter, 2 * quarter)):
        near_att = lax.all_gather(
            attended[:, at : at + wide], "seq", axis_index_groups=rows, tiled=True
        )
        weight_term = lax.dot_general(
            near_att, near_out, (((0,), (0,)), ((), ())), preferred_element_type=jnp.float32
        ).astype(jnp.bfloat16)
        weight_parts = lax.all_to_all(
            weight_term.reshape(wide, far, -1), "seq", 1, 0, axis_index_groups=columns
        )
        halves.append(jnp.sum(weight_parts.astype(jnp.float32), axis=0))
    grad_weight = jnp.concatenate(halves)
    grad_scores = (
        jnp.einsum("nthe,nshe->nhts", grad_blocks, value_blocks, preferred_element_type=jnp.float32)
        * factor
    )
    grad_probs = jnp.where(causal, grad_scores, 0.0).astype(jnp.bfloat16)
    grad_queries = jnp.einsum(
        "nhts,nshd->nthd", grad_probs, key_blocks, preferred_element_type=jnp.float32
    )
    grad_queries = grad_queries + factor * jnp.einsum(
        "nthe,nhde->nthd", grad_blocks, before, preferred_element_type=jnp.float32
    )
    grad_keys = jnp.einsum(
        "nhts,nthd->nshd", grad_probs, query_blocks, preferred_element_type=jnp.float32
    )
    grad_keys = grad_keys + factor * jnp.einsum(
        "nshe,nhde->nshd", value_blocks, after, preferred_element_type=jnp.float32
    )
    grad_values = jnp.einsum(
        "nhts,nthe->nshe", probs, grad_blocks, preferred_element_type=jnp.float32
    )
    grad_values = grad_values + factor * jnp.einsum(
        "nshd,nhde->nshe", key_blocks, after, preferred_element_type=jnp.float32
    )
    shape_out = (tokens_here, width_here)
    return (
        projected,
        grad_queries.astype(jnp.bfloat16).reshape(shape_out),
        grad_keys.astype(jnp.bfloat16).reshape(shape_out),
        grad_values.astype(jnp.bfloat16).reshape(shape_out),
        grad_weight,
    )


def solution(mesh):
    placed = (
        P("seq", "head"),
        P("seq", "head"),
        P("seq", "head"),
        P("seq"),
        P("head", None),
        P("seq", None),
    )
    return jax.shard_map(
        body,
        mesh=mesh,
        in_specs=placed,
        out_specs=(
            P("seq", "head"),
            P("seq", "head"),
            P("seq", "head"),
            P("seq", "head"),
            P("head", "seq"),
        ),
        check_vma=False,
    )
```

```python
import jax
import jax.numpy as jnp
from jax import lax
from jax.sharding import PartitionSpec as P

HD = 128
BLK = 128


def row_groups(count):
    near = 1
    while near * near < count:
        near += 1
    while count % near:
        near += 1
    far = count // near
    return near, far


def swapped(near, far, step):
    return [(r * near + c, r * near + (c ^ step)) for r in range(far) for c in range(near)]


def over_blocks(mask, states):
    count = states.shape[0]
    picked = [
        sum(mask[b, c] * states[c] for c in range(count) if c != b) + jnp.zeros_like(states[0])
        for b in range(count)
    ]
    return jnp.stack(picked)


def carried(states, grads, first_doc, last_doc):
    count, mine = (lax.axis_size("seq"), lax.axis_index("seq"))
    heads = states.shape[0]
    rows = heads * HD // count
    both = jnp.stack([states, grads]).astype(jnp.bfloat16).reshape(2, count, rows, HD)
    both = jnp.moveaxis(both, 1, 0)
    ends = jnp.stack([first_doc, last_doc]).astype(jnp.bfloat16)
    ends = jnp.broadcast_to(ends[None, :, None, None], (count, 2, 16, HD))
    got = lax.all_to_all(jnp.concatenate([both, ends], axis=2), "seq", 0, 0)
    firsts, lasts = (got[:, 0, rows, 0], got[:, 1, rows, 0])
    got = got[:, :, :rows]
    place = jnp.arange(count)
    ahead = ((lasts[None, :] == firsts[:, None]) & (place[None, :] < place[:, None])).astype(jnp.float32)
    behind = ((firsts[None, :] == lasts[:, None]) & (place[None, :] > place[:, None])).astype(jnp.float32)
    masks = jnp.stack([ahead, behind])
    summed = jnp.einsum(
        "kji,ikrd->jkrd", masks.astype(jnp.bfloat16), got, preferred_element_type=jnp.float32
    ).astype(jnp.bfloat16)
    back = lax.all_to_all(summed, "seq", 0, 0)
    back = jnp.moveaxis(back, 0, 1).reshape(2, heads, HD, HD).astype(jnp.float32)
    return back[0], back[1]


def body(queries, key_rows, value_rows, doc_block, out_weight, grad_output):
    factor = 1.0 / HD
    tokens_here = queries.shape[0]
    width_here = queries.shape[1]
    heads_here = width_here // HD
    block_count = tokens_here // BLK
    query_blocks = queries.reshape(block_count, BLK, heads_here, HD)
    key_blocks = key_rows.reshape(block_count, BLK, heads_here, HD)
    value_blocks = value_rows.reshape(block_count, BLK, heads_here, HD)
    near, far = row_groups(lax.axis_size("seq"))
    seat = lax.axis_index("seq") % near
    out_parts = grad_output.reshape(tokens_here, far, near, -1)

    def out_part(place):
        part = lax.dynamic_index_in_dim(out_parts, place, 2, keepdims=False)
        return part.reshape(tokens_here, -1)

    near_out = [out_part(seat)]
    for step in range(1, near):
        near_out.append(lax.ppermute(out_part(seat ^ step), "seq", swapped(near, far, step)))
    causal = jnp.tril(jnp.ones((BLK, BLK), dtype=bool))
    scores = (
        jnp.einsum("nthd,nshd->nhts", query_blocks, key_blocks, preferred_element_type=jnp.float32)
        * factor
    )
    probs = jnp.where(causal, scores, 0.0).astype(jnp.bfloat16)
    block_states = jnp.einsum(
        "nshd,nshe->nhde", key_blocks, value_blocks, preferred_element_type=jnp.float32
    )
    grad_att = lax.dot_general(
        grad_output, out_weight, (((1,), (1,)), ((), ())), preferred_element_type=jnp.float32
    ).astype(jnp.bfloat16)
    grad_blocks = grad_att.reshape(block_count, BLK, heads_here, HD)
    grad_states = jnp.einsum(
        "nthd,nthe->nhde", query_blocks, grad_blocks, preferred_element_type=jnp.float32
    )
    positions = jnp.arange(block_count, dtype=jnp.int32)
    same_doc = doc_block[:, None] == doc_block[None, :]
    earlier = (same_doc & (positions[None, :] < positions[:, None])).astype(jnp.float32)
    later = (same_doc & (positions[None, :] > positions[:, None])).astype(jnp.float32)
    last_doc = doc_block[block_count - 1]
    first_doc = doc_block[0]
    own_state = jnp.sum(
        jnp.where((doc_block == last_doc)[:, None, None, None], block_states, 0.0), axis=0
    )
    own_grad = jnp.sum(
        jnp.where((doc_block == first_doc)[:, None, None, None], grad_states, 0.0), axis=0
    )
    own_state, own_grad, near_out = lax.optimization_barrier((own_state, own_grad, near_out))
    carry_state, carry_grad = carried(own_state, own_grad, first_doc, last_doc)
    before = over_blocks(earlier, block_states)
    before = before + jnp.where(
        (doc_block == first_doc)[:, None, None, None], carry_state[None], 0.0
    )
    after = over_blocks(later, grad_states)
    after = after + jnp.where((doc_block == last_doc)[:, None, None, None], carry_grad[None], 0.0)
    before = before.astype(jnp.bfloat16)
    after = after.astype(jnp.bfloat16)
    attended = jnp.einsum(
        "nhts,nshe->nthe", probs, value_blocks, preferred_element_type=jnp.float32
    )
    attended = attended + factor * jnp.einsum("nthd,nhde->nthe", query_blocks, before, preferred_element_type=jnp.float32)
    attended = attended.astype(jnp.bfloat16).reshape(tokens_here, width_here)
    partial_value = jnp.dot(attended, out_weight, preferred_element_type=jnp.float32)
    partial_value = lax.optimization_barrier(partial_value.astype(jnp.bfloat16))
    projected = lax.psum_scatter(
        partial_value.astype(jnp.float32).astype(jnp.bfloat16),
        "head",
        scatter_dimension=1,
        tiled=True,
    )
    columns = [[r * near + c for r in range(far)] for c in range(near)]
    rows = [[r * near + c for c in range(near)] for r in range(far)]
    near_out = jnp.stack(near_out)
    near_out = jnp.concatenate(
        [lax.dynamic_index_in_dim(near_out, seat ^ c, 0, keepdims=False) for c in range(near)]
    )
    quarter = width_here // 4
    halves = []
    for at, wide in ((0, quarter), (quarter, quarter), (2 * quarter, 2 * quarter)):
        near_att = lax.all_gather(
            attended[:, at : at + wide], "seq", axis_index_groups=rows, tiled=True
        )
        weight_term = lax.dot_general(
            near_att, near_out, (((0,), (0,)), ((), ())), preferred_element_type=jnp.float32
        ).astype(jnp.bfloat16)
        weight_parts = lax.all_to_all(
            weight_term.reshape(wide, far, -1), "seq", 1, 0, axis_index_groups=columns
        )
        halves.append(jnp.sum(weight_parts.astype(jnp.float32), axis=0))
    grad_weight = jnp.concatenate(halves)
    grad_scores = (
        jnp.einsum("nthe,nshe->nhts", grad_blocks, value_blocks, preferred_element_type=jnp.float32)
        * factor
    )
    grad_probs = jnp.where(causal, grad_scores, 0.0).astype(jnp.bfloat16)
    grad_queries = jnp.einsum(
        "nhts,nshd->nthd", grad_probs, key_blocks, preferred_element_type=jnp.float32
    )
    grad_queries = grad_queries + factor * jnp.einsum(
        "nthe,nhde->nthd", grad_blocks, before, preferred_element_type=jnp.float32
    )
    grad_keys = jnp.einsum(
        "nhts,nthd->nshd", grad_probs, query_blocks, preferred_element_type=jnp.float32
    )
    grad_keys = grad_keys + factor * jnp.einsum(
        "nshe,nhde->nshd", value_blocks, after, preferred_element_type=jnp.float32
    )
    grad_values = jnp.einsum(
        "nhts,nthe->nshe", probs, grad_blocks, preferred_element_type=jnp.float32
    )
    grad_values = grad_values + factor * jnp.einsum(
        "nshd,nhde->nshe", key_blocks, after, preferred_element_type=jnp.float32
    )
    shape_out = (tokens_here, width_here)
    return (
        projected,
        grad_queries.astype(jnp.bfloat16).reshape(shape_out),
        grad_keys.astype(jnp.bfloat16).reshape(shape_out),
        grad_values.astype(jnp.bfloat16).reshape(shape_out),
        grad_weight,
    )


def solution(mesh):
    placed = (
        P("seq", "head"),
        P("seq", "head"),
        P("seq", "head"),
        P("seq"),
        P("head", None),
        P("seq", None),
    )
    return jax.shard_map(
        body,
        mesh=mesh,
        in_specs=placed,
        out_specs=(
            P("seq", "head"),
            P("seq", "head"),
            P("seq", "head"),
            P("seq", "head"),
            P("head", "seq"),
        ),
        check_vma=False,
    )
```
